32 devices in a mesh: dp: 2 (over core), context: 8 (over z, x), tensor: 2 (over y).
Axes of the slice: x: 2, y: 2, z: 4, core: 2. Of those that a mesh axis runs over, the one named last changes fastest.
Arguments:
- layer_input: bfloat16 [4, 1024, 1024], P('dp', 'context'), may hold values from -6 to 6
- segments: int32 [4, 1024], P('dp'), may hold values from 0 to 7, as said below
- w_qkv: bfloat16 [1024, 3, 1024], P(('dp', 'context'), None, 'tensor'), may hold values from -0.1875 to 0.1875
- bias_qv: bfloat16 [2, 2, 512], P(None, 'tensor', ('dp', 'context')), may hold values from -1.1953125 to 1.1953125
- w_out: bfloat16 [1024, 1024], P('tensor', ('dp', 'context')), may hold values from -3 to 3
- w_up: bfloat16 [1024, 4096], P(('dp', 'context'), 'tensor'), may hold values from -0.1875 to 0.1875
- bias_up: bfloat16 [2, 2048], P('tensor', ('dp', 'context')), may hold values from -1.1953125 to 1.1953125
- w_down: bfloat16 [4096, 1024], P('tensor', ('dp', 'context')), may hold values from -0.09375 to 0.09375
- norm_gains: bfloat16 [2, 1024], P(None, ('dp', 'context')), may hold values from 0.5 to 1.5
- shifts: bfloat16 [4, 1024], P(None, ('dp', 'context')), may hold values from -1.1953125 to 1.1953125
- cotangent: bfloat16 [4, 1024, 1024], P('dp', 'context'), may hold values from -6 to 6
Outputs:
- layer_output: bfloat16 [4, 1024, 1024], P('dp', 'context')
- grad_input: float32 [4, 1024, 1024], P('dp', 'context')
- grad_w_qkv: float32 [1024, 3, 1024], P(('dp', 'context'), None, 'tensor')
- grad_bias_qv: float32 [2, 2, 512], P(None, 'tensor', ('dp', 'context'))
- grad_w_out: float32 [1024, 1024], P('tensor', ('dp', 'context'))
- grad_w_up: float32 [1024, 4096], P(('dp', 'context'), 'tensor')
- grad_bias_up: float32 [2, 2048], P('tensor', ('dp', 'context'))
- grad_w_down: float32 [4096, 1024], P('tensor', ('dp', 'context'))
- grad_norm_gains: float32 [2, 1024], P(None, ('dp', 'context'))
- grad_shifts: float32 [4, 1024], P(None, ('dp', 'context'))
The draws below stay inside these ranges and needn't reach their ends.
Inputs may be any that keep to these rules, and one draw needn't show every extreme that they name: `segments`: segment numbers never fall along a row; in every aligned group of 2 rows one row, drawn from the seed, is a single segment.
All inputs are finite; a program needn't handle non-finite values.
Results may differ from the reference program's by a relative error of at most 0.012.
Values may be sent and summed in bfloat16 or wider, within the bound.
A program may use at most 448 MiB of HBM per device.

```python
import math
import jax
import jax.numpy as jnp
from jax import lax

D = 1024
HEADS = 16
FF = 4096
HEAD_DIM = 64
ROWS = 2
SEQ = 1024
NROWS = 4
N_TENSOR = 2


def draw_segments(key, part):
    key = jax.random.fold_in(key, 11)
    cut_key, row_key = jax.random.split(key)
    cuts = jax.random.randint(cut_key, (NROWS, 7), 1, SEQ)
    positions = jnp.arange(SEQ, dtype=jnp.int32)
    numbers = jnp.sum((positions[None, :, None] >= cuts[:, None, :]).astype(jnp.int32), axis=2)
    single = jax.random.randint(row_key, (NROWS // ROWS,), 0, ROWS)
    within = jnp.arange(NROWS, dtype=jnp.int32) % ROWS
    picked = within == jnp.repeat(single, ROWS)
    return jnp.where(picked[:, None], 0, numbers).astype(jnp.int32)


def block_levels(key, shape, pieces, least, top_value):
    def one(axis_at, parts):
        draws = jax.random.uniform(jax.random.fold_in(jax.random.fold_in(key, 6), axis_at), (parts,), jnp.float32, least / len(pieces), top_value / len(pieces))
        return jnp.repeat(jnp.exp(draws), shape[axis_at] // parts).reshape((-1,) + (1,) * (len(shape) - axis_at - 1))

    level = one(*pieces[0])
    for cut in pieces[1:]:
        level = level * one(*cut)
    return level


def centred(key, dims, deviation, reach, cuts=(), kind=jnp.bfloat16):
    result = deviation * jax.random.normal(key, dims, jnp.float32)
    if cuts:
        result = result * block_levels(key, dims, cuts, -0.22, 0.18)
    return jnp.clip(result, -reach, reach).astype(kind)


def setup_inputs(seed: int = 0) -> dict:
    key_of = jax.random.split(jax.random.key(seed), 12)
    layer_input = centred(key_of[0], (NROWS, SEQ, D), 1.0, 6.0, ((0, 2), (1, 8)))
    segments = draw_segments(jax.random.fold_in(key_of[11], 71), 0)
    w_qkv = centred(key_of[2], (D, 3, D), D ** -0.5, 0.1875, ((0, 16), (2, 2)))
    bias_qv = centred(key_of[3], (2, N_TENSOR, D // N_TENSOR), 0.2, 1.1953125, ((1, 2), (2, 16)))
    w_out = centred(key_of[4], (D, D), (D // 256) ** -0.5, 3.0, ((0, 2), (1, 16)))
    w_up = centred(key_of[5], (D, FF), D ** -0.5, 0.1875, ((0, 16), (1, 2)))
    bias_up = centred(key_of[6], (N_TENSOR, FF // N_TENSOR), 0.2, 1.1953125, ((0, 2), (1, 16)))
    w_down = centred(key_of[7], (FF, D), FF ** -0.5, 0.09375, ((0, 2), (1, 16)))
    norm_gains = jnp.clip(1.0 + 0.1 * jax.random.normal(key_of[8], (2, D), jnp.float32), 0.5, 1.5).astype(jnp.bfloat16)
    shifts = centred(key_of[9], (4, D), 0.2, 1.1953125, ((1, 16),))
    cotangent = centred(key_of[10], (NROWS, SEQ, D), 1.0, 6.0, ((0, 2), (1, 8)))
    return {"layer_input": layer_input, "segments": segments, "w_qkv": w_qkv, "bias_qv": bias_qv, "w_out": w_out, "w_up": w_up, "bias_up": bias_up, "w_down": w_down, "norm_gains": norm_gains, "shifts": shifts, "cotangent": cotangent}


@jax.custom_vjp
def low(v):
    return lax.optimization_barrier(v.astype(jnp.bfloat16)).astype(jnp.float32)

@jax.custom_vjp
def low_back(v):
    return v

def low_keep(v):
    return (low(v), None)

def low_pass(kept, grad):
    return (grad,)

def back_keep(v):
    return (v, None)

def back_low(kept, grad):
    return (low(grad),)
low.defvjp(low_keep, low_pass)
low_back.defvjp(back_keep, back_low)

def layer_norm(values, gain, shift):
    center = lax.optimization_barrier(jnp.mean(values, axis=-1, keepdims=True))
    shifted = values - center
    spread = lax.optimization_barrier(jnp.mean(shifted * shifted, axis=-1, keepdims=True))
    return shifted * lax.rsqrt(spread + 1e-05) * gain + shift

def attention(queries, keys, values, segment_row):
    block = math.gcd(SEQ, 512)
    head_scale = 1.0 / math.sqrt(HEAD_DIM)
    key_heads = keys.reshape(SEQ, HEADS, HEAD_DIM)
    value_heads = values.reshape(SEQ, HEADS, HEAD_DIM)
    positions = jnp.arange(SEQ, dtype=jnp.int32)

    def one_block(packed):
        query_block, begin = packed
        scores = jnp.einsum('qhd,khd->hqk', query_block, key_heads, precision=lax.Precision.HIGHEST) * head_scale
        scores = low_back(scores)
        query_pos = begin + jnp.arange(block, dtype=jnp.int32)
        query_seg = lax.dynamic_slice_in_dim(segment_row, begin, block, 0)
        mask = (query_pos[:, None] >= positions[None, :]) & (query_seg[:, None] == segment_row[None, :])
        scores = jnp.where(mask[None], scores, -1e+30)
        top = lax.optimization_barrier(jnp.max(scores, axis=-1, keepdims=True))
        weights = jnp.exp(scores - top)
        weights = weights / lax.optimization_barrier(jnp.sum(weights, axis=-1, keepdims=True))
        return jnp.einsum('hqk,khd->qhd', low(weights), value_heads, precision=lax.Precision.HIGHEST)
    query_blocks = queries.reshape(SEQ // block, block, HEADS, HEAD_DIM)
    begins = jnp.arange(SEQ // block, dtype=jnp.int32) * block
    return lax.map(jax.checkpoint(one_block), (query_blocks, begins)).reshape(SEQ, D)

def row_forward(params, row_input, segment_row):
    w_qkv, bias_qv, w_out, w_up, bias_up, w_down, norm_gains, shifts = params
    first = low(layer_norm(row_input, norm_gains[0], shifts[0]))
    projected = jnp.einsum('ld,dkf->lkf', first, w_qkv, precision=lax.Precision.HIGHEST)
    biases = bias_qv.reshape(2, D)
    queries = low(low_back(projected[:, 0] + biases[0]))
    keys = low(low_back(projected[:, 1]))
    values = low(low_back(projected[:, 2] + biases[1]))
    mixed = low(low_back(attention(queries, keys, values, segment_row)))
    branch = low_back(jnp.dot(mixed, w_out, precision=lax.Precision.HIGHEST) + shifts[2])
    hidden = row_input + branch
    second = low(layer_norm(hidden, norm_gains[1], shifts[1]))
    upward = low_back(jnp.dot(second, w_up, precision=lax.Precision.HIGHEST) + bias_up.reshape(FF))
    active = low(jax.nn.gelu(upward, approximate=True))
    return hidden + low_back(jnp.dot(active, w_down, precision=lax.Precision.HIGHEST) + shifts[3])

def reference(layer_input, segments, w_qkv, bias_qv, w_out, w_up, bias_up, w_down, norm_gains, shifts, cotangent):
    params = tuple((array.astype(jnp.float32) for array in (w_qkv, bias_qv, w_out, w_up, bias_up, w_down, norm_gains, shifts)))
    inputs = layer_input.astype(jnp.float32)

    def forward(weights, input_rows):

        def one_row(packed):
            return row_forward(weights, packed[0], packed[1])
        return lax.map(jax.checkpoint(one_row), (input_rows, segments))
    outputs, backward = jax.vjp(forward, params, inputs)
    param_grads, input_grad = backward(cotangent.astype(jnp.float32))
    return (outputs.astype(jnp.bfloat16), input_grad, param_grads[0], param_grads[1], param_grads[2], param_grads[3], param_grads[4], param_grads[5], param_grads[6], param_grads[7])
```

```python
from functools import partial
import math

import jax
import jax.numpy as jnp
from jax import lax
from jax.experimental import pallas as pl
from jax.experimental.pallas import tpu as pltpu
from jax.sharding import PartitionSpec as P

HEAD_DIM = 64


def normalize(values):
    center = jnp.mean(values, axis=-1, keepdims=True)
    shifted = values - center
    inverse = lax.rsqrt(jnp.mean(shifted * shifted, axis=-1, keepdims=True) + 1e-05)
    return (shifted * inverse, inverse)


def norm_back(grad, normed, inverse, gain):
    scaled = grad * gain
    return inverse * (
        scaled
        - jnp.mean(scaled, axis=-1, keepdims=True)
        - normed * jnp.mean(scaled * normed, axis=-1, keepdims=True)
    )


def split_heads(block_rows):
    return block_rows.reshape(block_rows.shape[0], -1, HEAD_DIM)


def masked_scores(queries, keys, query_seg, key_seg, query_pos, key_pos):
    scores = jnp.einsum(
        "qhd,khd->hqk", split_heads(queries), split_heads(keys), preferred_element_type=jnp.float32
    ) * (1.0 / math.sqrt(HEAD_DIM))
    mask = (query_pos[:, None] >= key_pos[None, :]) & (query_seg[:, None] == key_seg[None, :])
    return jnp.where(mask[None], scores, -1e30)


def general_shards(
    layer_input,
    segments,
    w_qkv,
    bias_qv,
    w_out,
    w_up,
    bias_up,
    w_down,
    norm_gains,
    shifts,
    cotangent,
):
    rows, span_len, width = layer_input.shape
    length = segments.shape[1]
    head_scale = 1.0 / math.sqrt(HEAD_DIM)
    begin = lax.axis_index("context") * span_len
    full_qkv, full_bias, full_out, full_up, full_upbias, full_down, gains, offsets = (
        lax.all_gather(w_qkv, ("dp", "context"), axis=0, tiled=True),
        lax.all_gather(bias_qv, ("dp", "context"), axis=2, tiled=True),
        lax.all_gather(w_out, ("dp", "context"), axis=1, tiled=True),
        lax.all_gather(w_up, ("dp", "context"), axis=0, tiled=True),
        lax.all_gather(bias_up, ("dp", "context"), axis=1, tiled=True),
        lax.all_gather(w_down, ("dp", "context"), axis=1, tiled=True),
        lax.all_gather(norm_gains, ("dp", "context"), axis=1, tiled=True),
        lax.all_gather(shifts, ("dp", "context"), axis=1, tiled=True),
    )
    gains = gains.astype(jnp.float32)
    offsets = offsets.astype(jnp.float32)
    query_pos = begin + jnp.arange(span_len, dtype=jnp.int32)
    key_pos = jnp.arange(length, dtype=jnp.int32)
    query_seg = lax.dynamic_slice_in_dim(segments, begin, span_len, 1)
    inputs = layer_input.astype(jnp.float32)
    normed_one, inverse_one = normalize(inputs)
    first = (normed_one * gains[0] + offsets[0]).astype(jnp.bfloat16)
    projected = jnp.einsum("rcd,dkf->rckf", first, full_qkv, preferred_element_type=jnp.float32)
    queries = (projected[:, :, 0] + full_bias[0, 0].astype(jnp.float32)).astype(jnp.bfloat16)
    keys = projected[:, :, 1].astype(jnp.bfloat16)
    values = (projected[:, :, 2] + full_bias[1, 0].astype(jnp.float32)).astype(jnp.bfloat16)
    key_rows, value_rows = (
        lax.all_gather(keys, "context", axis=1, tiled=True),
        lax.all_gather(values, "context", axis=1, tiled=True),
    )

    def forward_row(packed):
        query_row, key_row, value_row, seg_here, seg_all = packed
        scores = masked_scores(query_row, key_row, seg_here, seg_all, query_pos, key_pos)
        top = jnp.max(scores, axis=-1, keepdims=True)
        exponent = jnp.exp(scores - top)
        total = jnp.sum(exponent, axis=-1, keepdims=True)
        weights = exponent / total
        result_row = jnp.einsum(
            "hqk,khd->qhd",
            weights.astype(jnp.bfloat16),
            split_heads(value_row),
            preferred_element_type=jnp.float32,
        )
        return (result_row.reshape(span_len, -1), (top + jnp.log(total))[..., 0])

    mixed, log_totals = lax.map(forward_row, (queries, key_rows, value_rows, query_seg, segments))
    mixed = mixed.astype(jnp.bfloat16)
    branch = (
        lax.psum(
            jnp.einsum("rcf,fd->rcd", mixed, full_out, preferred_element_type=jnp.float32), "tensor"
        )
        + offsets[2]
    )
    hidden = inputs + branch
    normed_two, inverse_two = normalize(hidden)
    second = (normed_two * gains[1] + offsets[1]).astype(jnp.bfloat16)
    upward = jnp.einsum(
        "rcd,df->rcf", second, full_up, preferred_element_type=jnp.float32
    ) + full_upbias[0].astype(jnp.float32)
    active, gelu_back = jax.vjp(partial(jax.nn.gelu, approximate=True), upward)
    active_low = active.astype(jnp.bfloat16)
    down = (
        lax.psum(
            jnp.einsum(
                "rcf,fd->rcd", active_low, full_down, preferred_element_type=jnp.float32
            ).astype(jnp.bfloat16),
            "tensor",
        ).astype(jnp.float32)
        + offsets[3]
    )
    result = (hidden + down).astype(jnp.bfloat16)
    grad_out = cotangent.astype(jnp.float32)
    down_grad = jnp.einsum("rcf,rcd->fd", active_low, cotangent, preferred_element_type=jnp.float32)
    active_grad = jnp.einsum(
        "rcd,fd->rcf", cotangent, full_down, preferred_element_type=jnp.float32
    )
    up_grad = gelu_back(active_grad)[0].astype(jnp.bfloat16)
    upbias_grad = jnp.sum(up_grad, axis=(0, 1), dtype=jnp.float32)[None]
    upw_grad = jnp.einsum("rcd,rcf->df", second, up_grad, preferred_element_type=jnp.float32)
    second_grad = lax.psum(
        jnp.einsum("rcf,df->rcd", up_grad, full_up, preferred_element_type=jnp.float32), "tensor"
    )
    hidden_grad = grad_out + norm_back(second_grad, normed_two, inverse_two, gains[1])
    branch_low = hidden_grad.astype(jnp.bfloat16)
    outw_grad = jnp.einsum("rcf,rcd->fd", mixed, branch_low, preferred_element_type=jnp.float32)
    mixed_grad = jnp.einsum(
        "rcd,fd->rcf", branch_low, full_out, preferred_element_type=jnp.float32
    ).astype(jnp.bfloat16)

    def query_side(packed):
        query_row, key_row, value_row, seg_here, seg_all, grad_row, log_row = packed
        scores = masked_scores(query_row, key_row, seg_here, seg_all, query_pos, key_pos)
        weights = jnp.exp(scores - log_row[..., None])
        weight_grad = jnp.einsum(
            "qhd,khd->hqk",
            split_heads(grad_row),
            split_heads(value_row),
            preferred_element_type=jnp.float32,
        )
        inner = jnp.sum(weights * weight_grad, axis=-1)
        score_grad = (weights * (weight_grad - inner[..., None])).astype(jnp.bfloat16)
        query_grad = (
            jnp.einsum(
                "hqk,khd->qhd", score_grad, split_heads(key_row), preferred_element_type=jnp.float32
            )
            * head_scale
        ).reshape(span_len, -1)
        key_term = (
            jnp.einsum(
                "hqk,qhd->khd",
                score_grad,
                split_heads(query_row),
                preferred_element_type=jnp.float32,
            )
            * head_scale
        )
        value_term = jnp.einsum(
            "hqk,qhd->khd",
            weights.astype(jnp.bfloat16),
            split_heads(grad_row),
            preferred_element_type=jnp.float32,
        )
        return (query_grad, (key_term.reshape(length, -1), value_term.reshape(length, -1)))

    query_grad, extra = lax.map(
        query_side, (queries, key_rows, value_rows, query_seg, segments, mixed_grad, log_totals)
    )
    key_sum, value_sum = lax.psum_scatter(extra, "context", scatter_dimension=1, tiled=True)
    key_grad = key_sum.astype(jnp.bfloat16)
    value_grad = value_sum.astype(jnp.bfloat16)
    query_low = query_grad.astype(jnp.bfloat16)
    stacked_grads = jnp.stack([query_low, key_grad, value_grad], axis=2)
    qkv_grad = jnp.einsum("rcd,rckf->dkf", first, stacked_grads, preferred_element_type=jnp.float32)
    bias_grad = jnp.stack(
        [
            jnp.sum(query_low, axis=(0, 1), dtype=jnp.float32),
            jnp.sum(value_grad, axis=(0, 1), dtype=jnp.float32),
        ]
    )[:, None]
    first_grad = lax.psum(
        jnp.einsum(
            "rckf,dkf->rcd", stacked_grads, full_qkv, preferred_element_type=jnp.float32
        ).astype(jnp.bfloat16),
        "tensor",
    ).astype(jnp.float32)
    input_grad = hidden_grad + norm_back(first_grad, normed_one, inverse_one, gains[0])
    gain_grad = jnp.stack(
        [
            jnp.sum(first_grad * normed_one, axis=(0, 1)),
            jnp.sum(second_grad * normed_two, axis=(0, 1)),
        ]
    )
    offset_grad = jnp.stack(
        [
            jnp.sum(first_grad, axis=(0, 1)),
            jnp.sum(second_grad, axis=(0, 1)),
            jnp.sum(branch_low, axis=(0, 1), dtype=jnp.float32),
            jnp.sum(cotangent, axis=(0, 1), dtype=jnp.float32),
        ]
    )
    sent_qkv, sent_bias, sent_out, sent_up, sent_upbias, sent_down, sent_gain, sent_offset = (
        lax.psum_scatter(qkv_grad, ("dp", "context"), scatter_dimension=0, tiled=True),
        lax.psum_scatter(bias_grad, ("dp", "context"), scatter_dimension=2, tiled=True),
        lax.psum_scatter(outw_grad, ("dp", "context"), scatter_dimension=1, tiled=True),
        lax.psum_scatter(upw_grad, ("dp", "context"), scatter_dimension=0, tiled=True),
        lax.psum_scatter(upbias_grad, ("dp", "context"), scatter_dimension=1, tiled=True),
        lax.psum_scatter(down_grad, ("dp", "context"), scatter_dimension=1, tiled=True),
        lax.psum_scatter(gain_grad, ("dp", "context"), scatter_dimension=1, tiled=True),
        lax.psum_scatter(offset_grad, ("dp", "context"), scatter_dimension=1, tiled=True),
    )
    return (
        result,
        input_grad,
        sent_qkv,
        sent_bias,
        sent_out,
        sent_up,
        sent_upbias,
        sent_down,
        sent_gain,
        sent_offset,
    )


MESH = pl.DeviceIdType.MESH
VMEM_BYTES = 56 * 1024 * 1024


def other_z(z, step, count):
    if count == 4:
        return (z + 1 - 2 * (z % 2), (z + 2) % 4, 3 - z)[step - 1]
    return (z + step) % count


def place():
    d = lax.axis_index("dp")
    c = lax.axis_index("context")
    t = lax.axis_index("tensor")
    return d, c // 2, c % 2, t


def greet(peers):
    barrier = pltpu.get_barrier_semaphore()
    for peer in peers:
        pl.semaphore_signal(barrier, inc=1, device_id=peer, device_id_type=MESH)
    pl.semaphore_wait(barrier, len(peers))


def gather_kernel(arrays, nz, *refs):
    sources, results = refs[:arrays], refs[arrays : 2 * arrays]
    own_sem, send_sem, recv_sem = refs[2 * arrays :]
    d, z, x, t = place()
    nc = 2 * nz
    here = z * 2 + x
    peer_x = (d, z * 2 + 1 - x, t)
    peer_d = (1 - d, here, t)
    peers_z = [(d, other_z(z, k, nz) * 2 + x, t) for k in range(1, nz)]
    greet(peers_z + [peer_x, peer_d])
    pending = []

    def send(a, source, shard, slot, peer):
        copy = pltpu.make_async_remote_copy(
            src_ref=source,
            dst_ref=results[a].at[shard],
            send_sem=send_sem.at[a, slot],
            recv_sem=recv_sem.at[a, shard],
            device_id=peer,
            device_id_type=MESH,
        )
        copy.start()
        pending.append(copy)

    def arrived(a, shard):
        pltpu.make_async_remote_copy(
            src_ref=sources[a],
            dst_ref=results[a].at[shard],
            send_sem=send_sem.at[a, 0],
            recv_sem=recv_sem.at[a, shard],
            device_id=peer_d,
            device_id_type=MESH,
        ).wait_recv()

    mine = d * nc + here
    locals_ = []
    for a in range(arrays):
        for k in range(1, nz):
            send(a, sources[a], mine, k - 1, peers_z[k - 1])
        send(a, sources[a], mine, nz - 1, peer_x)
        send(a, sources[a], mine, 2 * nz - 1, peer_d)
        keep = pltpu.make_async_copy(sources[a], results[a].at[mine], own_sem.at[a])
        keep.start()
        locals_.append(keep)
    for a in range(arrays):
        for k in range(nz):
            row = z if k == 0 else other_z(z, k, nz)
            if k:
                shard = d * nc + row * 2 + x
                arrived(a, shard)
                send(a, results[a].at[shard], shard, nz - 1 + k, peer_x)
                send(a, results[a].at[shard], shard, 2 * nz - 1 + k, peer_d)
            shard = d * nc + row * 2 + 1 - x
            arrived(a, shard)
            send(a, results[a].at[shard], shard, 3 * nz - 1 + k, peer_d)
    for a in range(arrays):
        for k in range(nc):
            arrived(a, (1 - d) * nc + k)
        locals_[a].wait()
    for copy in pending:
        copy.wait_send()


def gather_weights(nc, *arrays):
    count = len(arrays)
    hbm = pl.BlockSpec(memory_space=pl.ANY)
    results = pl.pallas_call(
        partial(gather_kernel, count, nc // 2),
        out_shape=[jax.ShapeDtypeStruct((2 * nc,) + a.shape, a.dtype) for a in arrays],
        in_specs=[hbm] * count,
        out_specs=[hbm] * count,
        scratch_shapes=[
            pltpu.SemaphoreType.DMA((count,)),
            pltpu.SemaphoreType.DMA((count, 2 * nc - 1)),
            pltpu.SemaphoreType.DMA((count, 2 * nc)),
        ],
        compiler_params=pltpu.CompilerParams(collective_id=0, has_side_effects=True),
    )(*arrays)
    return [r.reshape((-1,) + r.shape[2:]) for r in results]


def exchange_kernel(nc, source, result, own_sem, send_sem, recv_sem):
    d, z, x, t = place()
    here = z * 2 + x
    greet([(d, (here + k) % nc, t) for k in range(1, nc)])
    keep = pltpu.make_async_copy(source.at[here], result.at[here], own_sem)
    keep.start()
    copies = []
    for k in range(1, nc):
        target = (here + k) % nc
        copy = pltpu.make_async_remote_copy(
            src_ref=source.at[target],
            dst_ref=result.at[here],
            send_sem=send_sem.at[k],
            recv_sem=recv_sem.at[k],
            device_id=(d, target, t),
            device_id_type=MESH,
        )
        copy.start()
        copies.append(copy)
    keep.wait()
    for k, copy in enumerate(copies, 1):
        copy.wait_send()
        pltpu.make_async_remote_copy(
            src_ref=source.at[here],
            dst_ref=result.at[(here + nc - k) % nc],
            send_sem=send_sem.at[k],
            recv_sem=recv_sem.at[k],
            device_id=(d, (here + k) % nc, t),
            device_id_type=MESH,
        ).wait_recv()


def exchange(blocks, which):
    nc = blocks.shape[0]
    hbm = pl.BlockSpec(memory_space=pl.ANY)
    return pl.pallas_call(
        partial(exchange_kernel, nc),
        out_shape=jax.ShapeDtypeStruct(blocks.shape, blocks.dtype),
        in_specs=[hbm],
        out_specs=hbm,
        scratch_shapes=[
            pltpu.SemaphoreType.DMA,
            pltpu.SemaphoreType.DMA((nc,)),
            pltpu.SemaphoreType.DMA((nc,)),
        ],
        compiler_params=pltpu.CompilerParams(collective_id=which, has_side_effects=True),
    )(blocks)


def scatter_kernel(arrays, nz, *refs):
    grads, results = refs[:arrays], refs[arrays : 2 * arrays]
    scratch = refs[2 * arrays :]
    from_d, to_x, from_x, to_z, from_z = (scratch[i * arrays : (i + 1) * arrays] for i in range(5))
    send_sem, recv_sem = scratch[5 * arrays :]
    d, z, x, t = place()
    nc = 2 * nz
    here = z * 2 + x
    peer_x = (d, z * 2 + 1 - x, t)
    peer_d = (1 - d, here, t)
    rows = [z if k == 0 else other_z(z, k, nz) for k in range(nz)]
    peers_z = [(d, rows[k] * 2 + x, t) for k in range(1, nz)]
    greet(peers_z + [peer_x, peer_d])
    pending = []

    def send(a, source, target, slot, peer):
        copy = pltpu.make_async_remote_copy(
            src_ref=source,
            dst_ref=target,
            send_sem=send_sem.at[a, slot],
            recv_sem=recv_sem.at[a, slot],
            device_id=peer,
            device_id_type=MESH,
        )
        copy.start()
        pending.append(copy)
        return copy

    def added(target, *terms):
        step = 16

        @pl.loop(0, target.shape[0] // step)
        def _(i):
            part = pl.ds(pl.multiple_of(i * step, step), step)
            total = terms[0][part].astype(jnp.float32)
            for term in terms[1:]:
                total = total + term[part].astype(jnp.float32)
            target[part] = total.astype(target.dtype)

    order = list(range(1, nz)) + [0]
    halves = [[], []]
    for a in range(arrays):
        first = {}
        for side in range(2):
            for k in order:
                column = 1 - x if side == 0 else x
                shard = rows[k] * 2 + column
                slot = side * nz + k
                first[slot] = send(
                    a, grads[a].at[(1 - d) * nc + shard], from_d[a].at[slot], slot, peer_d
                )
        halves[0].append(first)
    for a in range(arrays):
        second = {}
        for k in order:
            halves[0][a][k].wait_recv()
            added(
                to_x[a].at[k], grads[a].at[d * nc + rows[k] * 2 + 1 - x], from_d[a].at[k]
            )
            second[k] = send(a, to_x[a].at[k], from_x[a].at[k], nc + k, peer_x)
        halves[1].append(second)
    last = []
    for a in range(arrays):
        third = []
        for k in order:
            halves[0][a][nz + k].wait_recv()
            halves[1][a][k].wait_recv()
            if k:
                added(
                    to_z[a].at[k - 1],
                    grads[a].at[d * nc + rows[k] * 2 + x],
                    from_d[a].at[nz + k],
                    from_x[a].at[k],
                )
                back = (nz - k) if nz != 4 else k
                third.append(
                    send(a, to_z[a].at[k - 1], from_z[a].at[back - 1], nc + nz + k - 1, peers_z[k - 1])
                )
        last.append(third)
    for a in range(arrays):
        for copy in last[a]:
            copy.wait_recv()
        added(
            results[a],
            grads[a].at[d * nc + here],
            from_d[a].at[nz],
            from_x[a].at[0],
            *[from_z[a].at[k] for k in range(nz - 1)],
        )
    for copy in pending:
        copy.wait_send()


def scatter_grads(nc, *arrays):
    count = len(arrays)
    nz = nc // 2
    blocks = [a.reshape((2 * nc, -1, a.shape[-1])) for a in arrays]
    shapes = [b.shape[1:] for b in blocks]
    vmem = pl.BlockSpec(memory_space=pltpu.VMEM)

    def buffers(number):
        return [pltpu.VMEM((number,) + s, jnp.bfloat16) for s in shapes]

    return pl.pallas_call(
        partial(scatter_kernel, count, nz),
        out_shape=[jax.ShapeDtypeStruct(s, jnp.float32) for s in shapes],
        in_specs=[vmem] * count,
        out_specs=[vmem] * count,
        scratch_shapes=buffers(nc)
        + buffers(nz)
        + buffers(nz)
        + buffers(nz - 1)
        + buffers(nz - 1)
        + [
            pltpu.SemaphoreType.DMA((count, nc + 2 * nz - 1)),
            pltpu.SemaphoreType.DMA((count, nc + 2 * nz - 1)),
        ],
        compiler_params=pltpu.CompilerParams(
            collective_id=5, has_side_effects=True, vmem_limit_bytes=VMEM_BYTES
        ),
    )(*blocks)


def tensor_sum(part):
    low = part.astype(jnp.bfloat16)
    other = lax.ppermute(low, "tensor", [(0, 1), (1, 0)])
    return low.astype(jnp.float32) + other.astype(jnp.float32)


def head_shards(
    layer_input,
    segments,
    w_qkv,
    bias_qv,
    w_out,
    w_up,
    bias_up,
    w_down,
    norm_gains,
    shifts,
    cotangent,
):
    rows, span, width = layer_input.shape
    length = segments.shape[1]
    share = w_qkv.shape[0]
    features = w_qkv.shape[2]
    hidden_units = w_up.shape[1]
    nc = length // span
    devices = 2 * nc
    head_scale = 1.0 / math.sqrt(HEAD_DIM)
    f32, low_type = jnp.float32, jnp.bfloat16
    small = jnp.concatenate(
        [norm_gains.T, shifts.T, bias_qv.reshape(share, -1), bias_up.reshape(share, -1)], axis=1
    )
    small = jnp.pad(small, ((0, 0), (0, 128 - small.shape[1])))
    full_qkv, full_small, out_t, full_up, down_t = gather_weights(
        nc, w_qkv.reshape(share, -1), small, w_out.T, w_up, w_down.T
    )
    gains = full_small[:, 0:2].T.astype(f32)
    offsets = full_small[:, 2:6].T.astype(f32)
    biases = full_small[:, 6].reshape(devices, 2, -1).transpose(1, 0, 2).reshape(2, features).astype(f32)
    upbias = full_small[:, 7:9].reshape(-1).astype(f32)
    bias_col = jnp.concatenate([biases[0], jnp.zeros_like(biases[0]), biases[1]])

    inputs = layer_input.astype(f32)
    normed_one, inverse_one = normalize(inputs)
    first = (normed_one * gains[0] + offsets[0]).astype(low_type)
    projected = jnp.einsum("dn,rcd->nrc", full_qkv, first, preferred_element_type=f32)
    projected = (projected + bias_col[:, None, None]).astype(low_type)
    sent = projected.reshape(3, nc, HEAD_DIM, rows, span).transpose(1, 3, 0, 2, 4)
    qkv = exchange(sent, 1).transpose(1, 2, 3, 0, 4).reshape(rows, 3, HEAD_DIM, length)
    queries, keys, values = qkv[:, 0], qkv[:, 1], qkv[:, 2]
    position = jnp.arange(length, dtype=jnp.int32)
    mask = (position[:, None] >= position[None, :])[None] & (
        segments[:, :, None] == segments[:, None, :]
    )
    scores = jnp.einsum("rfi,rfj->rij", queries, keys, preferred_element_type=f32) * head_scale
    scores = jnp.where(mask, scores, -1e30)
    top = jnp.max(scores, axis=-1, keepdims=True)
    exponent = jnp.exp(scores - top)
    weights = exponent / jnp.sum(exponent, axis=-1, keepdims=True)
    weights_low = weights.astype(low_type)
    mixed = jnp.einsum("rfj,rij->rfi", values, weights_low, preferred_element_type=f32)
    mixed = mixed.astype(low_type).reshape(rows, HEAD_DIM, nc, span).transpose(2, 0, 1, 3)
    mixed = exchange(mixed, 2).transpose(1, 3, 0, 2).reshape(rows, span, features)

    branch = (
        tensor_sum(jnp.einsum("rcf,df->rcd", mixed, out_t, preferred_element_type=f32)) + offsets[2]
    )
    hidden = inputs + branch
    normed_two, inverse_two = normalize(hidden)
    second = (normed_two * gains[1] + offsets[1]).astype(low_type)
    upward = jnp.einsum("rcd,df->rcf", second, full_up, preferred_element_type=f32) + upbias
    active, gelu_back = jax.vjp(partial(jax.nn.gelu, approximate=True), upward)
    active_low = active.astype(low_type)
    down = (
        tensor_sum(jnp.einsum("rcf,df->rcd", active_low, down_t, preferred_element_type=f32))
        + offsets[3]
    )
    result = (hidden + down).astype(low_type)
    grad_out = cotangent.astype(f32)
    down_grad = jnp.einsum("rcd,rcf->df", cotangent, active_low, preferred_element_type=f32)
    active_grad = jnp.einsum("rcd,df->rcf", cotangent, down_t, preferred_element_type=f32)
    up_grad = gelu_back(active_grad)[0].astype(low_type)
    upbias_grad = jnp.sum(up_grad, axis=(0, 1), dtype=f32)
    second_grad = tensor_sum(
        jnp.einsum("rcf,df->rcd", up_grad, full_up, preferred_element_type=f32)
    )
    upw_grad = jnp.einsum("rcd,rcf->df", second, up_grad, preferred_element_type=f32)
    hidden_grad = grad_out + norm_back(second_grad, normed_two, inverse_two, gains[1])
    branch_low = hidden_grad.astype(low_type)
    mixed_grad = jnp.einsum("df,rcd->frc", out_t, branch_low, preferred_element_type=f32)
    mixed_grad = mixed_grad.astype(low_type).reshape(nc, HEAD_DIM, rows, span).transpose(0, 2, 1, 3)
    mixed_grad = exchange(mixed_grad, 3).transpose(1, 2, 0, 3).reshape(rows, HEAD_DIM, length)
    outw_grad = jnp.einsum("rcd,rcf->df", branch_low, mixed, preferred_element_type=f32)

    weight_grad = jnp.einsum("rfi,rfj->rij", mixed_grad, values, preferred_element_type=f32)
    inner = jnp.sum(weights * weight_grad, axis=-1, keepdims=True)
    score_grad = (weights * (weight_grad - inner)).astype(low_type)
    query_grad = (
        jnp.einsum("rfj,rij->rfi", keys, score_grad, preferred_element_type=f32) * head_scale
    )
    key_grad = (
        jnp.einsum("rfi,rij->rfj", queries, score_grad, preferred_element_type=f32) * head_scale
    )
    value_grad = jnp.einsum("rfi,rij->rfj", mixed_grad, weights_low, preferred_element_type=f32)
    stacked = jnp.stack([query_grad, key_grad, value_grad], axis=1).astype(low_type)
    stacked = stacked.reshape(rows, 3, HEAD_DIM, nc, span).transpose(3, 0, 1, 2, 4)
    stacked = exchange(stacked, 4).transpose(1, 4, 2, 0, 3).reshape(rows, span, 3 * features)

    first_grad = tensor_sum(
        jnp.einsum("rcn,dn->rcd", stacked, full_qkv, preferred_element_type=f32)
    )
    qkv_grad = jnp.einsum("rcd,rcn->dn", first, stacked, preferred_element_type=f32)
    input_grad = hidden_grad + norm_back(first_grad, normed_one, inverse_one, gains[0])
    sums = jnp.sum(stacked, axis=(0, 1), dtype=f32).reshape(3, devices, -1)
    bias_grad = jnp.concatenate([sums[0], sums[2]], axis=1).reshape(-1, 1)
    small_grad = jnp.concatenate(
        [
            jnp.stack(
                [
                    jnp.sum(first_grad * normed_one, axis=(0, 1)),
                    jnp.sum(second_grad * normed_two, axis=(0, 1)),
                    jnp.sum(first_grad, axis=(0, 1)),
                    jnp.sum(second_grad, axis=(0, 1)),
                    jnp.sum(branch_low, axis=(0, 1), dtype=f32),
                    jnp.sum(cotangent, axis=(0, 1), dtype=f32),
                ],
                axis=1,
            ),
            bias_grad,
            upbias_grad.reshape(width, -1),
        ],
        axis=1,
    )
    small_grad = jnp.pad(small_grad, ((0, 0), (0, 128 - small_grad.shape[1])))
    sent_down, sent_up, sent_out, sent_qkv, sent_small = scatter_grads(
        nc,
        *[g.astype(low_type) for g in (down_grad, upw_grad, outw_grad, qkv_grad, small_grad)],
    )
    return (
        result,
        input_grad,
        sent_qkv.reshape(w_qkv.shape),
        sent_small[:, 6].reshape(bias_qv.shape),
        sent_out.T,
        sent_up,
        sent_small[:, 7:9].reshape(bias_up.shape),
        sent_down.T,
        sent_small[:, 0:2].T,
        sent_small[:, 2:6].T,
    )


def shards(layer_input, segments, w_qkv, *rest):
    contexts = segments.shape[1] // layer_input.shape[1]
    by_heads = (
        contexts * HEAD_DIM == w_qkv.shape[2]
        and w_qkv.shape[0] == 64
        and layer_input.shape[1] % 128 == 0
        and contexts % 2 == 0
    )
    chosen = head_shards if by_heads else general_shards
    return chosen(layer_input, segments, w_qkv, *rest)


def solution(mesh):
    return jax.shard_map(
        shards,
        mesh=mesh,
        in_specs=(
            P("dp", "context", None),
            P("dp", None),
            P(("dp", "context"), None, "tensor"),
            P(None, "tensor", ("dp", "context")),
            P("tensor", ("dp", "context")),
            P(("dp", "context"), "tensor"),
            P("tensor", ("dp", "context")),
            P("tensor", ("dp", "context")),
            P(None, ("dp", "context")),
            P(None, ("dp", "context")),
            P("dp", "context", None),
        ),
        out_specs=(
            P("dp", "context", None),
            P("dp", "context", None),
            P(("dp", "context"), None, "tensor"),
            P(None, "tensor", ("dp", "context")),
            P("tensor", ("dp", "context")),
            P(("dp", "context"), "tensor"),
            P("tensor", ("dp", "context")),
            P("tensor", ("dp", "context")),
            P(None, ("dp", "context")),
            P(None, ("dp", "context")),
        ),
        check_vma=False,
    )
```

```python
from functools import partial
import math

import jax
import jax.numpy as jnp
from jax import lax
from jax.experimental import pallas as pl
from jax.experimental.pallas import tpu as pltpu
from jax.sharding import PartitionSpec as P

HEAD_DIM = 64


def normalize(values):
    center = jnp.mean(values, axis=-1, keepdims=True)
    shifted = values - center
    inverse = lax.rsqrt(jnp.mean(shifted * shifted, axis=-1, keepdims=True) + 1e-05)
    return (shifted * inverse, inverse)


def norm_back(grad, normed, inverse, gain):
    scaled = grad * gain
    return inverse * (
        scaled
        - jnp.mean(scaled, axis=-1, keepdims=True)
        - normed * jnp.mean(scaled * normed, axis=-1, keepdims=True)
    )


def split_heads(block_rows):
    return block_rows.reshape(block_rows.shape[0], -1, HEAD_DIM)


def masked_scores(queries, keys, query_seg, key_seg, query_pos, key_pos):
    scores = jnp.einsum(
        "qhd,khd->hqk", split_heads(queries), split_heads(keys), preferred_element_type=jnp.float32
    ) * (1.0 / math.sqrt(HEAD_DIM))
    mask = (query_pos[:, None] >= key_pos[None, :]) & (query_seg[:, None] == key_seg[None, :])
    return jnp.where(mask[None], scores, -1e30)


def general_shards(
    layer_input,
    segments,
    w_qkv,
    bias_qv,
    w_out,
    w_up,
    bias_up,
    w_down,
    norm_gains,
    shifts,
    cotangent,
):
    rows, span_len, width = layer_input.shape
    length = segments.shape[1]
    head_scale = 1.0 / math.sqrt(HEAD_DIM)
    begin = lax.axis_index("context") * span_len
    full_qkv, full_bias, full_out, full_up, full_upbias, full_down, gains, offsets = (
        lax.all_gather(w_qkv, ("dp", "context"), axis=0, tiled=True),
        lax.all_gather(bias_qv, ("dp", "context"), axis=2, tiled=True),
        lax.all_gather(w_out, ("dp", "context"), axis=1, tiled=True),
        lax.all_gather(w_up, ("dp", "context"), axis=0, tiled=True),
        lax.all_gather(bias_up, ("dp", "context"), axis=1, tiled=True),
        lax.all_gather(w_down, ("dp", "context"), axis=1, tiled=True),
        lax.all_gather(norm_gains, ("dp", "context"), axis=1, tiled=True),
        lax.all_gather(shifts, ("dp", "context"), axis=1, tiled=True),
    )
    gains = gains.astype(jnp.float32)
    offsets = offsets.astype(jnp.float32)
    query_pos = begin + jnp.arange(span_len, dtype=jnp.int32)
    key_pos = jnp.arange(length, dtype=jnp.int32)
    query_seg = lax.dynamic_slice_in_dim(segments, begin, span_len, 1)
    inputs = layer_input.astype(jnp.float32)
    normed_one, inverse_one = normalize(inputs)
    first = (normed_one * gains[0] + offsets[0]).astype(jnp.bfloat16)
    projected = jnp.einsum("rcd,dkf->rckf", first, full_qkv, preferred_element_type=jnp.float32)
    queries = (projected[:, :, 0] + full_bias[0, 0].astype(jnp.float32)).astype(jnp.bfloat16)
    keys = projected[:, :, 1].astype(jnp.bfloat16)
    values = (projected[:, :, 2] + full_bias[1, 0].astype(jnp.float32)).astype(jnp.bfloat16)
    key_rows, value_rows = (
        lax.all_gather(keys, "context", axis=1, tiled=True),
        lax.all_gather(values, "context", axis=1, tiled=True),
    )

    def forward_row(packed):
        query_row, key_row, value_row, seg_here, seg_all = packed
        scores = masked_scores(query_row, key_row, seg_here, seg_all, query_pos, key_pos)
        top = jnp.max(scores, axis=-1, keepdims=True)
        exponent = jnp.exp(scores - top)
        total = jnp.sum(exponent, axis=-1, keepdims=True)
        weights = exponent / total
        result_row = jnp.einsum(
            "hqk,khd->qhd",
            weights.astype(jnp.bfloat16),
            split_heads(value_row),
            preferred_element_type=jnp.float32,
        )
        return (result_row.reshape(span_len, -1), (top + jnp.log(total))[..., 0])

    mixed, log_totals = lax.map(forward_row, (queries, key_rows, value_rows, query_seg, segments))
    mixed = mixed.astype(jnp.bfloat16)
    branch = (
        lax.psum(
            jnp.einsum("rcf,fd->rcd", mixed, full_out, preferred_element_type=jnp.float32), "tensor"
        )
        + offsets[2]
    )
    hidden = inputs + branch
    normed_two, inverse_two = normalize(hidden)
    second = (normed_two * gains[1] + offsets[1]).astype(jnp.bfloat16)
    upward = jnp.einsum(
        "rcd,df->rcf", second, full_up, preferred_element_type=jnp.float32
    ) + full_upbias[0].astype(jnp.float32)
    active, gelu_back = jax.vjp(partial(jax.nn.gelu, approximate=True), upward)
    active_low = active.astype(jnp.bfloat16)
    down = (
        lax.psum(
            jnp.einsum(
                "rcf,fd->rcd", active_low, full_down, preferred_element_type=jnp.float32
            ).astype(jnp.bfloat16),
            "tensor",
        ).astype(jnp.float32)
        + offsets[3]
    )
    result = (hidden + down).astype(jnp.bfloat16)
    grad_out = cotangent.astype(jnp.float32)
    down_grad = jnp.einsum("rcf,rcd->fd", active_low, cotangent, preferred_element_type=jnp.float32)
    active_grad = jnp.einsum(
        "rcd,fd->rcf", cotangent, full_down, preferred_element_type=jnp.float32
    )
    up_grad = gelu_back(active_grad)[0].astype(jnp.bfloat16)
    upbias_grad = jnp.sum(up_grad, axis=(0, 1), dtype=jnp.float32)[None]
    upw_grad = jnp.einsum("rcd,rcf->df", second, up_grad, preferred_element_type=jnp.float32)
    second_grad = lax.psum(
        jnp.einsum("rcf,df->rcd", up_grad, full_up, preferred_element_type=jnp.float32), "tensor"
    )
    hidden_grad = grad_out + norm_back(second_grad, normed_two, inverse_two, gains[1])
    branch_low = hidden_grad.astype(jnp.bfloat16)
    outw_grad = jnp.einsum("rcf,rcd->fd", mixed, branch_low, preferred_element_type=jnp.float32)
    mixed_grad = jnp.einsum(
        "rcd,fd->rcf", branch_low, full_out, preferred_element_type=jnp.float32
    ).astype(jnp.bfloat16)

    def query_side(packed):
        query_row, key_row, value_row, seg_here, seg_all, grad_row, log_row = packed
        scores = masked_scores(query_row, key_row, seg_here, seg_all, query_pos, key_pos)
        weights = jnp.exp(scores - log_row[..., None])
        weight_grad = jnp.einsum(
            "qhd,khd->hqk",
            split_heads(grad_row),
            split_heads(value_row),
            preferred_element_type=jnp.float32,
        )
        inner = jnp.sum(weights * weight_grad, axis=-1)
        score_grad = (weights * (weight_grad - inner[..., None])).astype(jnp.bfloat16)
        query_grad = (
            jnp.einsum(
                "hqk,khd->qhd", score_grad, split_heads(key_row), preferred_element_type=jnp.float32
            )
            * head_scale
        ).reshape(span_len, -1)
        key_term = (
            jnp.einsum(
                "hqk,qhd->khd",
                score_grad,
                split_heads(query_row),
                preferred_element_type=jnp.float32,
            )
            * head_scale
        )
        value_term = jnp.einsum(
            "hqk,qhd->khd",
            weights.astype(jnp.bfloat16),
            split_heads(grad_row),
            preferred_element_type=jnp.float32,
        )
        return (query_grad, (key_term.reshape(length, -1), value_term.reshape(length, -1)))

    query_grad, extra = lax.map(
        query_side, (queries, key_rows, value_rows, query_seg, segments, mixed_grad, log_totals)
    )
    key_sum, value_sum = lax.psum_scatter(extra, "context", scatter_dimension=1, tiled=True)
    key_grad = key_sum.astype(jnp.bfloat16)
    value_grad = value_sum.astype(jnp.bfloat16)
    query_low = query_grad.astype(jnp.bfloat16)
    stacked_grads = jnp.stack([query_low, key_grad, value_grad], axis=2)
    qkv_grad = jnp.einsum("rcd,rckf->dkf", first, stacked_grads, preferred_element_type=jnp.float32)
    bias_grad = jnp.stack(
        [
            jnp.sum(query_low, axis=(0, 1), dtype=jnp.float32),
            jnp.sum(value_grad, axis=(0, 1), dtype=jnp.float32),
        ]
    )[:, None]
    first_grad = lax.psum(
        jnp.einsum(
            "rckf,dkf->rcd", stacked_grads, full_qkv, preferred_element_type=jnp.float32
        ).astype(jnp.bfloat16),
        "tensor",
    ).astype(jnp.float32)
    input_grad = hidden_grad + norm_back(first_grad, normed_one, inverse_one, gains[0])
    gain_grad = jnp.stack(
        [
            jnp.sum(first_grad * normed_one, axis=(0, 1)),
            jnp.sum(second_grad * normed_two, axis=(0, 1)),
        ]
    )
    offset_grad = jnp.stack(
        [
            jnp.sum(first_grad, axis=(0, 1)),
            jnp.sum(second_grad, axis=(0, 1)),
            jnp.sum(branch_low, axis=(0, 1), dtype=jnp.float32),
            jnp.sum(cotangent, axis=(0, 1), dtype=jnp.float32),
        ]
    )
    sent_qkv, sent_bias, sent_out, sent_up, sent_upbias, sent_down, sent_gain, sent_offset = (
        lax.psum_scatter(qkv_grad, ("dp", "context"), scatter_dimension=0, tiled=True),
        lax.psum_scatter(bias_grad, ("dp", "context"), scatter_dimension=2, tiled=True),
        lax.psum_scatter(outw_grad, ("dp", "context"), scatter_dimension=1, tiled=True),
        lax.psum_scatter(upw_grad, ("dp", "context"), scatter_dimension=0, tiled=True),
        lax.psum_scatter(upbias_grad, ("dp", "context"), scatter_dimension=1, tiled=True),
        lax.psum_scatter(down_grad, ("dp", "context"), scatter_dimension=1, tiled=True),
        lax.psum_scatter(gain_grad, ("dp", "context"), scatter_dimension=1, tiled=True),
        lax.psum_scatter(offset_grad, ("dp", "context"), scatter_dimension=1, tiled=True),
    )
    return (
        result,
        input_grad,
        sent_qkv,
        sent_bias,
        sent_out,
        sent_up,
        sent_upbias,
        sent_down,
        sent_gain,
        sent_offset,
    )


MESH = pl.DeviceIdType.MESH
VMEM_BYTES = 56 * 1024 * 1024
CHUNK = 1024
AHEAD = 2


def other_z(z, step, count):
    if count == 4:
        return (z + 1 - 2 * (z % 2), (z + 2) % 4, 3 - z)[step - 1]
    return (z + step) % count


def place():
    d = lax.axis_index("dp")
    c = lax.axis_index("context")
    t = lax.axis_index("tensor")
    return d, c // 2, c % 2, t


def greet(peers):
    barrier = pltpu.get_barrier_semaphore()
    for peer in peers:
        pl.semaphore_signal(barrier, inc=1, device_id=peer, device_id_type=MESH)
    pl.semaphore_wait(barrier, len(peers))


def column_chunks(widths):
    chunks = []
    for a, width in enumerate(widths):
        pieces = -(-width // CHUNK)
        for p in range(pieces):
            chunks.append((a, p * (width // pieces), width // pieces))
    return chunks


def gather_kernel(chunks, arrays, nz, *refs):
    sources, results = refs[:arrays], refs[arrays : 2 * arrays]
    own_sem, send_sem, recv_sem = refs[2 * arrays :]
    d, z, x, t = place()
    nc = 2 * nz
    here = z * 2 + x
    mine = d * nc + here
    peer_x = (d, z * 2 + 1 - x, t)
    peer_d = (1 - d, here, t)
    peers_z = [(d, other_z(z, k, nz) * 2 + x, t) for k in range(1, nz)]
    greet(peers_z + [peer_x, peer_d])
    pending = []

    def source(q):
        a, begin, size = chunks[q]
        return sources[a].at[:, pl.ds(begin, size)]

    def landing(q, shard):
        a, begin, size = chunks[q]
        return results[a].at[shard, :, pl.ds(begin, size)]

    def send(q, origin, shard, slot, peer):
        copy = pltpu.make_async_remote_copy(
            src_ref=origin,
            dst_ref=landing(q, shard),
            send_sem=send_sem.at[q, slot],
            recv_sem=recv_sem.at[q, shard],
            device_id=peer,
            device_id_type=MESH,
        )
        copy.start()
        pending.append(copy)

    def arrived(q, shard):
        pltpu.make_async_remote_copy(
            src_ref=source(q),
            dst_ref=landing(q, shard),
            send_sem=send_sem.at[q, 0],
            recv_sem=recv_sem.at[q, shard],
            device_id=peer_d,
            device_id_type=MESH,
        ).wait_recv()

    def begin_chunk(q):
        for k in range(1, nz):
            send(q, source(q), mine, k - 1, peers_z[k - 1])
        send(q, source(q), mine, nz - 1, peer_x)
        send(q, source(q), mine, 2 * nz - 1, peer_d)

    def across(q):
        for k in range(1, nz):
            shard = d * nc + other_z(z, k, nz) * 2 + x
            arrived(q, shard)
            send(q, landing(q, shard), shard, nz - 1 + k, peer_x)
            send(q, landing(q, shard), shard, 2 * nz - 1 + k, peer_d)

    def inward(q):
        for k in range(nz):
            row = z if k == 0 else other_z(z, k, nz)
            shard = d * nc + row * 2 + 1 - x
            arrived(q, shard)
            send(q, landing(q, shard), shard, 3 * nz - 1 + k, peer_d)

    count = len(chunks)
    begin_chunk(0)
    keeps = []
    for a in range(arrays):
        keep = pltpu.make_async_copy(sources[a], results[a].at[mine], own_sem.at[a])
        keep.start()
        keeps.append(keep)
    for q in range(1, min(AHEAD, count)):
        begin_chunk(q)
    for q in range(count + 1):
        if q < count:
            across(q)
            if q + AHEAD < count:
                begin_chunk(q + AHEAD)
        if q >= 1:
            inward(q - 1)
    for q in range(count):
        for k in range(nc):
            arrived(q, (1 - d) * nc + k)
    for keep in keeps:
        keep.wait()
    for copy in pending:
        copy.wait_send()


def gather_weights(nc, *arrays):
    count = len(arrays)
    chunks = column_chunks([a.shape[1] for a in arrays])
    hbm = pl.BlockSpec(memory_space=pl.ANY)
    results = pl.pallas_call(
        partial(gather_kernel, chunks, count, nc // 2),
        out_shape=[jax.ShapeDtypeStruct((2 * nc,) + a.shape, a.dtype) for a in arrays],
        in_specs=[hbm] * count,
        out_specs=[hbm] * count,
        scratch_shapes=[
            pltpu.SemaphoreType.DMA((count,)),
            pltpu.SemaphoreType.DMA((len(chunks), 2 * nc - 1)),
            pltpu.SemaphoreType.DMA((len(chunks), 2 * nc)),
        ],
        compiler_params=pltpu.CompilerParams(collective_id=0, has_side_effects=True),
    )(*arrays)
    return [r.reshape((-1,) + r.shape[2:]) for r in results]


def exchange_kernel(nc, source, result, own_sem, send_sem, recv_sem):
    d, z, x, t = place()
    here = z * 2 + x
    greet([(d, (here + k) % nc, t) for k in range(1, nc)])
    keep = pltpu.make_async_copy(source.at[here], result.at[here], own_sem)
    keep.start()
    copies = []
    for k in range(1, nc):
        target = (here + k) % nc
        copy = pltpu.make_async_remote_copy(
            src_ref=source.at[target],
            dst_ref=result.at[here],
            send_sem=send_sem.at[k],
            recv_sem=recv_sem.at[k],
            device_id=(d, target, t),
            device_id_type=MESH,
        )
        copy.start()
        copies.append(copy)
    keep.wait()
    for k, copy in enumerate(copies, 1):
        copy.wait_send()
        pltpu.make_async_remote_copy(
            src_ref=source.at[here],
            dst_ref=result.at[(here + nc - k) % nc],
            send_sem=send_sem.at[k],
            recv_sem=recv_sem.at[k],
            device_id=(d, (here + k) % nc, t),
            device_id_type=MESH,
        ).wait_recv()


def exchange(blocks, which):
    nc = blocks.shape[0]
    hbm = pl.BlockSpec(memory_space=pl.ANY)
    return pl.pallas_call(
        partial(exchange_kernel, nc),
        out_shape=jax.ShapeDtypeStruct(blocks.shape, blocks.dtype),
        in_specs=[hbm],
        out_specs=hbm,
        scratch_shapes=[
            pltpu.SemaphoreType.DMA,
            pltpu.SemaphoreType.DMA((nc,)),
            pltpu.SemaphoreType.DMA((nc,)),
        ],
        compiler_params=pltpu.CompilerParams(collective_id=which, has_side_effects=True),
    )(blocks)


def scatter_kernel(chunks, arrays, nz, *refs):
    grads, results = refs[:arrays], refs[arrays : 2 * arrays]
    scratch = refs[2 * arrays :]
    count = len(chunks)
    from_d, to_x, from_x, to_z, from_z = (scratch[i * count : (i + 1) * count] for i in range(5))
    send_sem, recv_sem = scratch[5 * count :]
    d, z, x, t = place()
    nc = 2 * nz
    here = z * 2 + x
    peer_x = (d, z * 2 + 1 - x, t)
    peer_d = (1 - d, here, t)
    rows = [z if k == 0 else other_z(z, k, nz) for k in range(nz)]
    peers_z = [(d, rows[k] * 2 + x, t) for k in range(1, nz)]
    greet(peers_z + [peer_x, peer_d])
    pending = []

    def grad(q, shard):
        a, begin, size = chunks[q]
        return grads[a].at[shard, :, pl.ds(begin, size)]

    def send(q, source, target, slot, peer):
        copy = pltpu.make_async_remote_copy(
            src_ref=source,
            dst_ref=target,
            send_sem=send_sem.at[q, slot],
            recv_sem=recv_sem.at[q, slot],
            device_id=peer,
            device_id_type=MESH,
        )
        copy.start()
        pending.append(copy)
        return copy

    def added(target, *terms):
        step = 16

        @pl.loop(0, target.shape[0] // step)
        def _(i):
            part = pl.ds(pl.multiple_of(i * step, step), step)
            total = terms[0][part].astype(jnp.float32)
            for term in terms[1:]:
                total = total + term[part].astype(jnp.float32)
            target[part] = total.astype(target.dtype)

    order = list(range(1, nz)) + [0]
    first, second, third = {}, {}, {}

    def inward(q):
        for side in range(2):
            for k in order:
                column = 1 - x if side == 0 else x
                slot = side * nz + k
                first[q, slot] = send(
                    q,
                    grad(q, (1 - d) * nc + rows[k] * 2 + column),
                    from_d[q].at[slot],
                    slot,
                    peer_d,
                )

    def across(q):
        for k in order:
            first[q, k].wait_recv()
            added(to_x[q].at[k], grad(q, d * nc + rows[k] * 2 + 1 - x), from_d[q].at[k])
            second[q, k] = send(q, to_x[q].at[k], from_x[q].at[k], nc + k, peer_x)

    def along(q):
        for k in order:
            first[q, nz + k].wait_recv()
            second[q, k].wait_recv()
            if k:
                added(
                    to_z[q].at[k - 1],
                    grad(q, d * nc + rows[k] * 2 + x),
                    from_d[q].at[nz + k],
                    from_x[q].at[k],
                )
                back = (nz - k) if nz != 4 else k
                third[q, back] = send(
                    q, to_z[q].at[k - 1], from_z[q].at[back - 1], nc + nz + back - 1, peers_z[k - 1]
                )

    def finish(q):
        for k in range(1, nz):
            third[q, k].wait_recv()
        a, begin, size = chunks[q]
        added(
            results[a].at[:, pl.ds(begin, size)],
            grad(q, d * nc + here),
            from_d[q].at[nz],
            from_x[q].at[0],
            *[from_z[q].at[k] for k in range(nz - 1)],
        )

    for q in range(min(AHEAD, count)):
        inward(q)
    for q in range(count + 4):
        if q + AHEAD < count:
            inward(q + AHEAD)
        if q < count:
            across(q)
        if 0 <= q - 2 < count:
            along(q - 2)
        if 0 <= q - 4 < count:
            finish(q - 4)
    for copy in pending:
        copy.wait_send()


def scatter_grads(nc, *arrays):
    count = len(arrays)
    nz = nc // 2
    blocks = [a.reshape((2 * nc, -1, a.shape[-1])) for a in arrays]
    share = blocks[0].shape[1]
    chunks = column_chunks([b.shape[2] for b in blocks])
    vmem = pl.BlockSpec(memory_space=pltpu.VMEM)

    def buffers(number):
        return [pltpu.VMEM((number, share, size), jnp.bfloat16) for _, _, size in chunks]

    return pl.pallas_call(
        partial(scatter_kernel, chunks, count, nz),
        out_shape=[jax.ShapeDtypeStruct(b.shape[1:], jnp.float32) for b in blocks],
        in_specs=[vmem] * count,
        out_specs=[vmem] * count,
        scratch_shapes=buffers(nc)
        + buffers(nz)
        + buffers(nz)
        + buffers(nz - 1)
        + buffers(nz - 1)
        + [
            pltpu.SemaphoreType.DMA((len(chunks), nc + 2 * nz - 1)),
            pltpu.SemaphoreType.DMA((len(chunks), nc + 2 * nz - 1)),
        ],
        compiler_params=pltpu.CompilerParams(
            collective_id=5, has_side_effects=True, vmem_limit_bytes=VMEM_BYTES
        ),
    )(*blocks)


def tensor_sum(part):
    low = part.astype(jnp.bfloat16)
    other = lax.ppermute(low, "tensor", [(0, 1), (1, 0)])
    return low.astype(jnp.float32) + other.astype(jnp.float32)


def head_shards(
    layer_input,
    segments,
    w_qkv,
    bias_qv,
    w_out,
    w_up,
    bias_up,
    w_down,
    norm_gains,
    shifts,
    cotangent,
):
    rows, span, width = layer_input.shape
    length = segments.shape[1]
    share = w_qkv.shape[0]
    features = w_qkv.shape[2]
    hidden_units = w_up.shape[1]
    nc = length // span
    devices = 2 * nc
    head_scale = 1.0 / math.sqrt(HEAD_DIM)
    f32, low_type = jnp.float32, jnp.bfloat16
    small = jnp.concatenate(
        [norm_gains.T, shifts.T, bias_qv.reshape(share, -1), bias_up.reshape(share, -1)], axis=1
    )
    small = jnp.pad(small, ((0, 0), (0, 128 - small.shape[1])))
    full_qkv, full_small, out_t, full_up, down_t = gather_weights(
        nc, w_qkv.reshape(share, -1), small, w_out.T, w_up, w_down.T
    )
    gains = full_small[:, 0:2].T.astype(f32)
    offsets = full_small[:, 2:6].T.astype(f32)
    biases = full_small[:, 6].reshape(devices, 2, -1).transpose(1, 0, 2).reshape(2, features).astype(f32)
    upbias = full_small[:, 7:9].reshape(-1).astype(f32)
    bias_col = jnp.concatenate([biases[0], jnp.zeros_like(biases[0]), biases[1]])

    inputs = layer_input.astype(f32)
    normed_one, inverse_one = normalize(inputs)
    first = (normed_one * gains[0] + offsets[0]).astype(low_type)
    projected = jnp.einsum("dn,rcd->nrc", full_qkv, first, preferred_element_type=f32)
    projected = (projected + bias_col[:, None, None]).astype(low_type)
    sent = projected.reshape(3, nc, HEAD_DIM, rows, span).transpose(1, 3, 0, 2, 4)
    qkv = exchange(sent, 1).transpose(1, 2, 3, 0, 4).reshape(rows, 3, HEAD_DIM, length)
    queries, keys, values = qkv[:, 0], qkv[:, 1], qkv[:, 2]
    position = jnp.arange(length, dtype=jnp.int32)
    mask = (position[:, None] >= position[None, :])[None] & (
        segments[:, :, None] == segments[:, None, :]
    )
    scores = jnp.einsum("rfi,rfj->rij", queries, keys, preferred_element_type=f32) * head_scale
    scores = jnp.where(mask, scores, -1e30)
    top = jnp.max(scores, axis=-1, keepdims=True)
    exponent = jnp.exp(scores - top)
    weights = exponent / jnp.sum(exponent, axis=-1, keepdims=True)
    weights_low = weights.astype(low_type)
    mixed = jnp.einsum("rfj,rij->rfi", values, weights_low, preferred_element_type=f32)
    mixed = mixed.astype(low_type).reshape(rows, HEAD_DIM, nc, span).transpose(2, 0, 1, 3)
    mixed = exchange(mixed, 2).transpose(1, 3, 0, 2).reshape(rows, span, features)

    branch = (
        tensor_sum(jnp.einsum("rcf,df->rcd", mixed, out_t, preferred_element_type=f32)) + offsets[2]
    )
    hidden = inputs + branch
    normed_two, inverse_two = normalize(hidden)
    second = (normed_two * gains[1] + offsets[1]).astype(low_type)
    upward = jnp.einsum("rcd,df->rcf", second, full_up, preferred_element_type=f32) + upbias
    active, gelu_back = jax.vjp(partial(jax.nn.gelu, approximate=True), upward)
    active_low = active.astype(low_type)
    down = (
        tensor_sum(jnp.einsum("rcf,df->rcd", active_low, down_t, preferred_element_type=f32))
        + offsets[3]
    )
    result = (hidden + down).astype(low_type)
    grad_out = cotangent.astype(f32)
    down_grad = jnp.einsum("rcd,rcf->df", cotangent, active_low, preferred_element_type=f32)
    active_grad = jnp.einsum("rcd,df->rcf", cotangent, down_t, preferred_element_type=f32)
    up_grad = gelu_back(active_grad)[0].astype(low_type)
    upbias_grad = jnp.sum(up_grad, axis=(0, 1), dtype=f32)
    second_grad = tensor_sum(
        jnp.einsum("rcf,df->rcd", up_grad, full_up, preferred_element_type=f32)
    )
    upw_grad = jnp.einsum("rcd,rcf->df", second, up_grad, preferred_element_type=f32)
    hidden_grad = grad_out + norm_back(second_grad, normed_two, inverse_two, gains[1])
    branch_low = hidden_grad.astype(low_type)
    mixed_grad = jnp.einsum("df,rcd->frc", out_t, branch_low, preferred_element_type=f32)
    mixed_grad = mixed_grad.astype(low_type).reshape(nc, HEAD_DIM, rows, span).transpose(0, 2, 1, 3)
    mixed_grad = exchange(mixed_grad, 3).transpose(1, 2, 0, 3).reshape(rows, HEAD_DIM, length)
    outw_grad = jnp.einsum("rcd,rcf->df", branch_low, mixed, preferred_element_type=f32)

    weight_grad = jnp.einsum("rfi,rfj->rij", mixed_grad, values, preferred_element_type=f32)
    inner = jnp.sum(weights * weight_grad, axis=-1, keepdims=True)
    score_grad = (weights * (weight_grad - inner)).astype(low_type)
    query_grad = (
        jnp.einsum("rfj,rij->rfi", keys, score_grad, preferred_element_type=f32) * head_scale
    )
    key_grad = (
        jnp.einsum("rfi,rij->rfj", queries, score_grad, preferred_element_type=f32) * head_scale
    )
    value_grad = jnp.einsum("rfi,rij->rfj", mixed_grad, weights_low, preferred_element_type=f32)
    stacked = jnp.stack([query_grad, key_grad, value_grad], axis=1).astype(low_type)
    stacked = stacked.reshape(rows, 3, HEAD_DIM, nc, span).transpose(3, 0, 1, 2, 4)
    stacked = exchange(stacked, 4).transpose(1, 4, 2, 0, 3).reshape(rows, span, 3 * features)

    first_grad = tensor_sum(
        jnp.einsum("rcn,dn->rcd", stacked, full_qkv, preferred_element_type=f32)
    )
    qkv_grad = jnp.einsum("rcd,rcn->dn", first, stacked, preferred_element_type=f32)
    input_grad = hidden_grad + norm_back(first_grad, normed_one, inverse_one, gains[0])
    sums = jnp.sum(stacked, axis=(0, 1), dtype=f32).reshape(3, devices, -1)
    bias_grad = jnp.concatenate([sums[0], sums[2]], axis=1).reshape(-1, 1)
    small_grad = jnp.concatenate(
        [
            jnp.stack(
                [
                    jnp.sum(first_grad * normed_one, axis=(0, 1)),
                    jnp.sum(second_grad * normed_two, axis=(0, 1)),
                    jnp.sum(first_grad, axis=(0, 1)),
                    jnp.sum(second_grad, axis=(0, 1)),
                    jnp.sum(branch_low, axis=(0, 1), dtype=f32),
                    jnp.sum(cotangent, axis=(0, 1), dtype=f32),
                ],
                axis=1,
            ),
            bias_grad,
            upbias_grad.reshape(width, -1),
        ],
        axis=1,
    )
    small_grad = jnp.pad(small_grad, ((0, 0), (0, 128 - small_grad.shape[1])))
    sent_down, sent_up, sent_out, sent_qkv, sent_small = scatter_grads(
        nc,
        *[g.astype(low_type) for g in (down_grad, upw_grad, outw_grad, qkv_grad, small_grad)],
    )
    return (
        result,
        input_grad,
        sent_qkv.reshape(w_qkv.shape),
        sent_small[:, 6].reshape(bias_qv.shape),
        sent_out.T,
        sent_up,
        sent_small[:, 7:9].reshape(bias_up.shape),
        sent_down.T,
        sent_small[:, 0:2].T,
        sent_small[:, 2:6].T,
    )


def shards(layer_input, segments, w_qkv, *rest):
    contexts = segments.shape[1] // layer_input.shape[1]
    by_heads = (
        contexts * HEAD_DIM == w_qkv.shape[2]
        and w_qkv.shape[0] == 64
        and layer_input.shape[1] % 128 == 0
        and contexts % 2 == 0
    )
    chosen = head_shards if by_heads else general_shards
    return chosen(layer_input, segments, w_qkv, *rest)


def solution(mesh):
    return jax.shard_map(
        shards,
        mesh=mesh,
        in_specs=(
            P("dp", "context", None),
            P("dp", None),
            P(("dp", "context"), None, "tensor"),
            P(None, "tensor", ("dp", "context")),
            P("tensor", ("dp", "context")),
            P(("dp", "context"), "tensor"),
            P("tensor", ("dp", "context")),
            P("tensor", ("dp", "context")),
            P(None, ("dp", "context")),
            P(None, ("dp", "context")),
            P("dp", "context", None),
        ),
        out_specs=(
            P("dp", "context", None),
            P("dp", "context", None),
            P(("dp", "context"), None, "tensor"),
            P(None, "tensor", ("dp", "context")),
            P("tensor", ("dp", "context")),
            P(("dp", "context"), "tensor"),
            P("tensor", ("dp", "context")),
            P("tensor", ("dp", "context")),
            P(None, ("dp", "context")),
            P(None, ("dp", "context")),
        ),
        check_vma=False,
    )
```
